32 devices in a mesh: head: 1, tok: 8 (over z, core), hid: 4 (over y, x).
Axes of the slice: x: 2, y: 2, z: 4, core: 2. Of those that a mesh axis runs over, the one named last changes fastest.
Arguments:
- queries: bfloat16 [4096, 1024], P('tok', 'head'), may hold values from -12 to 12
- keys: bfloat16 [4096, 1024], P('tok', 'head'), may hold values from -12 to 12
- values: bfloat16 [4096, 1024], P('tok', 'head'), may hold values from -12 to 12
- token_rate: float32 [4096, 2], P('tok', 'head'), may hold values from 0.05 to 1
- head_rate: float32 [2], P('head'), may hold values from 0.2 to 1
- w_gate: bfloat16 [2, 512, 1024], P('head', None, 'hid'), may hold values from -0.25 to 0.25
- w_up: bfloat16 [2, 512, 1024], P('head', None, 'hid'), may hold values from -0.25 to 0.25
- w_down: bfloat16 [2, 1024, 512], P('head', 'hid'), may hold values from -0.25 to 0.25
Outputs:
- result: bfloat16 [4096, 1024], P('tok', ('head', 'hid'))
The draws below stay inside these ranges and needn't reach their ends.
All inputs are finite; a program needn't handle non-finite values.
Results may differ from the reference program's by a relative error of at most 0.035.
Values may be sent and summed in bfloat16 or wider, within the bound.
A program may use at most 64 MiB of HBM per device.

```python
import math
import jax
import jax.numpy as jnp
from jax import lax

DH = 512
FH = 1024
NS_ITERS = 3
HEADS = 2
TOKENS = 4096
N_HID = 4


def offset_vector(base_key, salt):
    sign_key, size_key = jax.random.split(jax.random.fold_in(base_key, salt), 2)
    amplitude = 0.3 * (16384.0 / TOKENS) ** 0.25
    signs = jnp.where(jax.random.bernoulli(sign_key, 0.5, (HEADS * DH,)), 1.0, -1.0)
    sizes = jax.random.uniform(size_key, (HEADS * DH,), minval=0.5, maxval=1.5)
    return (signs * sizes * amplitude).astype(jnp.float32)


def channel_draw(base_key, shift):
    first_key, second_key = jax.random.split(base_key, 2)
    channel = (jnp.arange(HEADS * DH) % DH).astype(jnp.float32)
    jitter = jnp.exp(jax.random.uniform(second_key, (HEADS * DH,), minval=math.log(0.7), maxval=math.log(1.4)))
    ramp = 10.0 ** (0.5 * channel / DH - 0.25)
    basic = jax.random.truncated_normal(first_key, -4.0, 4.0, (TOKENS, HEADS * DH))
    return jnp.clip(basic * ramp * jitter + shift[None, :], -12.0, 12.0).astype(jnp.bfloat16)


def draw_queries(key, part):
    return channel_draw(jax.random.fold_in(key, 37), offset_vector(key, 5))


def draw_keys(key, part):
    return channel_draw(jax.random.fold_in(key, 11), offset_vector(key, 5))


def draw_values(key, part):
    return channel_draw(jax.random.fold_in(key, 23), offset_vector(key, 7))


def strengthened(array, own_key, source, target, parts, factor):
    owner, partner = [(jnp.arange(array.shape[position]) // (array.shape[position] // parts)).reshape([-1 if axis == position else 1 for axis in range(array.ndim)]) for position in (source, target)]
    chosen = jax.random.permutation(own_key, parts)[partner]
    strong = (owner == chosen) | (owner == (partner + parts // 2) % parts)
    return jnp.where(strong, factor * array, array)


def block_scale(stream_key, shape, cuts, least, largest):
    loudness, own = 1.0, jax.random.fold_in(stream_key, 6)
    for dim, blocks in cuts:
        steps = jnp.exp(jax.random.uniform(jax.random.fold_in(own, dim), (blocks,), jnp.float32, least / len(cuts), largest / len(cuts)))
        loudness = loudness * jnp.repeat(steps, shape[dim] // blocks).reshape([-1 if axis == dim else 1 for axis in range(len(shape))])
    return loudness


def gaussian(key, extent, spread, limit, cuts=(), kind=jnp.bfloat16):
    entries = spread * jax.random.normal(key, extent, jnp.float32)
    if cuts:
        entries = entries * block_scale(key, extent, cuts, -0.22, 0.18)
    return jnp.clip(entries, -limit, limit).astype(kind)


def bell_draw_with(key, dims, deviation, reach, shards, heavy, kind=jnp.bfloat16):
    values = deviation * jax.random.normal(key, dims, jnp.float32)
    if shards:
        values = values * block_scale(key, dims, shards, -0.22, 0.18)
    return jnp.clip(strengthened(values, jax.random.fold_in(key, 3), *heavy), -reach, reach).astype(kind)


def setup_inputs(seed: int = 0) -> dict:
    seeds = jax.random.split(jax.random.key(seed), 9)
    return {
        "queries": draw_queries(jax.random.fold_in(seeds[8], 71), 0),
        "keys": draw_keys(jax.random.fold_in(seeds[8], 71), 0),
        "values": draw_values(jax.random.fold_in(seeds[8], 71), 0),
        "token_rate": jnp.clip(jnp.exp(math.log(1.0) - 2.9957323 * jax.random.uniform(seeds[3], (TOKENS, HEADS), jnp.float32) ** block_scale(seeds[3], (TOKENS, HEADS), ((0, 8),), -0.2, 0.2)), 0.05, 1.0),
        "head_rate": jnp.clip(jnp.exp(jax.random.uniform(seeds[4], (HEADS,), jnp.float32, math.log(0.2), math.log(1.0))), 0.2, 1.0),
        "w_gate": gaussian(seeds[5], (HEADS, DH, FH), DH ** -0.5, 0.25, ((2, 4),)),
        "w_up": gaussian(seeds[6], (HEADS, DH, FH), DH ** -0.5, 0.25, ((2, 4),)),
        "w_down": bell_draw_with(seeds[7], (HEADS, FH, DH), FH ** -0.5, 0.25, ((1, 4),), (1, 2, 4, 2.0)),
    }


poly_a = 3.4445
poly_b = -4.775
poly_c = 2.0315

def newton_schulz(iterate):
    for sweep_index in range(NS_ITERS):
        gram_full = jnp.dot(iterate, iterate.T, preferred_element_type=jnp.float32).astype(jnp.bfloat16)
        product = jnp.dot(gram_full, iterate, preferred_element_type=jnp.float32).astype(jnp.bfloat16)
        second = jnp.dot(gram_full, product, preferred_element_type=jnp.float32)
        iterate = (poly_a * iterate.astype(jnp.float32) + poly_b * product.astype(jnp.float32) + poly_c * second).astype(jnp.bfloat16)
    return iterate

def orthogonal(gradient):
    norm_value = jnp.sqrt(jnp.sum(gradient * gradient))
    return newton_schulz((gradient / (norm_value + 1e-07)).astype(jnp.bfloat16))

def rescale(fresh, previous, which_dim):
    old_norm = jnp.sqrt(lax.optimization_barrier(jnp.sum(jnp.square(previous.astype(jnp.float32)), axis=which_dim, keepdims=True)))
    new_norm = jnp.sqrt(lax.optimization_barrier(jnp.sum(fresh * fresh, axis=which_dim, keepdims=True)) + 1e-06)
    return (fresh * old_norm / new_norm).astype(jnp.bfloat16)

def one_head(query_part, key_part, value_part, rate_col, step_rate, gate_weight, up_weight, down_weight):
    gate_pre = jnp.dot(key_part, gate_weight, preferred_element_type=jnp.float32)
    up_pre = jnp.dot(key_part, up_weight, preferred_element_type=jnp.float32)
    gate_sig = jax.nn.sigmoid(gate_pre)
    active = gate_pre * gate_sig
    hidden_keys = (active * up_pre).astype(jnp.bfloat16)
    target = (-(rate_col[:, None] * value_part.astype(jnp.float32))).astype(jnp.bfloat16)
    back_hidden = jnp.dot(target, down_weight.T, preferred_element_type=jnp.float32)
    grad_gate = (back_hidden * up_pre * gate_sig * (1.0 + gate_pre * (1.0 - gate_sig))).astype(jnp.bfloat16)
    grad_up = (back_hidden * active).astype(jnp.bfloat16)
    term_gate = jnp.dot(key_part.T, grad_gate, preferred_element_type=jnp.float32)
    term_up = jnp.dot(key_part.T, grad_up, preferred_element_type=jnp.float32)
    term_down = jnp.dot(target.T, hidden_keys, preferred_element_type=jnp.float32)
    ortho_gate = orthogonal(term_gate)
    ortho_up = orthogonal(term_up)
    ortho_down = orthogonal(term_down)
    gate_new = rescale(gate_weight.astype(jnp.float32) - step_rate * ortho_gate.astype(jnp.float32), gate_weight, 0)
    up_new = rescale(up_weight.astype(jnp.float32) - step_rate * ortho_up.astype(jnp.float32), up_weight, 0)
    down_new = rescale(down_weight.astype(jnp.float32) - step_rate * ortho_down.T.astype(jnp.float32), down_weight, 1)
    query_gate = jnp.dot(query_part, gate_new, preferred_element_type=jnp.float32)
    query_up = jnp.dot(query_part, up_new, preferred_element_type=jnp.float32)
    query_hidden = (jax.nn.silu(query_gate) * query_up).astype(jnp.bfloat16)
    block_units = FH // N_HID
    pieces = jnp.einsum('tbf,bfd->btd', query_hidden.reshape(-1, N_HID, block_units).astype(jnp.float32), down_new.reshape(N_HID, block_units, DH).astype(jnp.float32))
    rounded = lax.optimization_barrier(pieces.astype(jnp.bfloat16))
    return lax.optimization_barrier(jnp.sum(rounded.astype(jnp.float32), axis=0)).astype(jnp.bfloat16)

def reference(queries, keys, values, token_rate, head_rate, w_gate, w_up, w_down):
    outputs = []
    for head_index in range(HEADS):
        low_col = head_index * DH
        outputs.append(one_head(queries[:, low_col:low_col + DH], keys[:, low_col:low_col + DH], values[:, low_col:low_col + DH], token_rate[:, head_index], head_rate[head_index], w_gate[head_index], w_up[head_index], w_down[head_index]))
    return jnp.concatenate(outputs, axis=1)
```

```python
import jax
import jax.numpy as jnp
from jax import lax
from jax.sharding import PartitionSpec as P

NS_ITERS = 3


poly_a = 3.4445
poly_b = -4.775
poly_c = 2.0315


def rescale(fresh, previous, which_dim):
    old_norm = jnp.sqrt(
        jnp.sum(jnp.square(previous.astype(jnp.float32)), axis=which_dim, keepdims=True)
    )
    new_norm = jnp.sqrt(jnp.sum(fresh * fresh, axis=which_dim, keepdims=True) + 1e-06)
    return (fresh * old_norm / new_norm).astype(jnp.bfloat16)


def local_sweeps(iterate):
    for sweep_index in range(NS_ITERS):
        gram_full = jnp.dot(iterate, iterate.T, preferred_element_type=jnp.float32).astype(
            jnp.bfloat16
        )
        product = jnp.dot(gram_full, iterate, preferred_element_type=jnp.float32).astype(
            jnp.bfloat16
        )
        second = jnp.dot(gram_full, product, preferred_element_type=jnp.float32)
        iterate = (
            poly_a * iterate.astype(jnp.float32)
            + poly_b * product.astype(jnp.float32)
            + poly_c * second
        ).astype(jnp.bfloat16)
    return iterate


def local(queries, keys, values, token_rate, head_rate, w_gate, w_up, w_down):
    tok_rows, all_cols = keys.shape
    heads_here = token_rate.shape[1]
    head_width = all_cols // heads_here
    unit_count = w_gate.shape[2]
    problems = 3 * heads_here
    key_rows = keys.reshape(tok_rows, heads_here, head_width)
    value_rows = values.reshape(tok_rows, heads_here, head_width)
    query_rows = queries.reshape(tok_rows, heads_here, head_width)
    gate_pre = jnp.einsum("thd,hdf->thf", key_rows, w_gate, preferred_element_type=jnp.float32)
    up_pre = jnp.einsum("thd,hdf->thf", key_rows, w_up, preferred_element_type=jnp.float32)
    gate_sig = jax.nn.sigmoid(gate_pre)
    active = gate_pre * gate_sig
    hidden_keys = (active * up_pre).astype(jnp.bfloat16)
    target = (-(token_rate[:, :, None] * value_rows.astype(jnp.float32))).astype(jnp.bfloat16)
    back_hidden = jnp.einsum("thd,hfd->thf", target, w_down, preferred_element_type=jnp.float32)
    grad_gate = (back_hidden * up_pre * gate_sig * (1.0 + gate_pre * (1.0 - gate_sig))).astype(
        jnp.bfloat16
    )
    grad_up = (back_hidden * active).astype(jnp.bfloat16)
    term_gate = jnp.einsum("thc,thf->chf", key_rows, grad_gate, preferred_element_type=jnp.float32)
    term_up = jnp.einsum("thc,thf->chf", key_rows, grad_up, preferred_element_type=jnp.float32)
    term_down = jnp.einsum("thc,thf->chf", target, hidden_keys, preferred_element_type=jnp.float32)
    ranks = lax.axis_size("tok")
    each = -(-problems // ranks)
    terms = jnp.stack((term_gate, term_up, term_down), axis=0).astype(jnp.bfloat16)
    terms = terms.transpose(2, 0, 1, 3).reshape(problems, head_width, unit_count)
    terms = jnp.pad(terms, ((0, each * ranks - problems), (0, 0), (0, 0)))
    summed = lax.psum_scatter(terms, "tok", scatter_dimension=0, tiled=True)
    complete = lax.all_gather(summed, "hid", axis=0)
    col_start = lax.axis_index("hid") * unit_count
    pieces = []
    for slot in range(each):
        whole = jnp.concatenate([complete[j, slot] for j in range(complete.shape[0])], axis=1)
        whole = whole.astype(jnp.float32)
        norm = jnp.sqrt(jnp.sum(whole * whole))
        mine = local_sweeps((whole / (norm + 1e-07)).astype(jnp.bfloat16))
        pieces.append(lax.dynamic_slice_in_dim(mine, col_start, unit_count, 1))
    gathered = lax.all_gather(jnp.stack(pieces, axis=0), "tok", axis=0, tiled=True)
    ortho_full = gathered[:problems].reshape(heads_here, 3, head_width, unit_count)
    step_rate = head_rate[:, None, None]
    gate_new = rescale(
        w_gate.astype(jnp.float32) - step_rate * ortho_full[:, 0].astype(jnp.float32), w_gate, 1
    )
    up_new = rescale(
        w_up.astype(jnp.float32) - step_rate * ortho_full[:, 1].astype(jnp.float32), w_up, 1
    )
    down_new = rescale(
        w_down.astype(jnp.float32)
        - step_rate * jnp.swapaxes(ortho_full[:, 2], 1, 2).astype(jnp.float32),
        w_down,
        2,
    )
    query_gate = jnp.einsum(
        "thd,hdf->thf", query_rows, gate_new, preferred_element_type=jnp.float32
    )
    query_up = jnp.einsum("thd,hdf->thf", query_rows, up_new, preferred_element_type=jnp.float32)
    query_hidden = (jax.nn.silu(query_gate) * query_up).astype(jnp.bfloat16)
    partial_value = jnp.einsum(
        "thf,hfd->thd", query_hidden, down_new, preferred_element_type=jnp.float32
    ).reshape(tok_rows, all_cols)
    return lax.psum_scatter(
        partial_value.astype(jnp.bfloat16), "hid", scatter_dimension=1, tiled=True
    )


def solution(mesh):
    return jax.shard_map(
        local,
        mesh=mesh,
        in_specs=(
            P("tok", "head"),
            P("tok", "head"),
            P("tok", "head"),
            P("tok", "head"),
            P("head"),
            P("head", None, "hid"),
            P("head", None, "hid"),
            P("head", "hid", None),
        ),
        out_specs=P("tok", ("head", "hid")),
        check_vma=False,
    )
```

```python
import functools
import jax
import jax.numpy as jnp
from jax import lax
from jax.experimental import pallas as pl
from jax.experimental.pallas import tpu as pltpu
from jax.sharding import PartitionSpec as P

NS_ITERS = 3
poly_a = 3.4445
poly_b = -4.775
poly_c = 2.0315
CHUNKS = 2
TOK_CHUNKS = 2
F32 = jnp.float32
BF16 = jnp.bfloat16
MESH = pl.DeviceIdType.MESH


def mm(x, y):
    return jnp.dot(x, y, preferred_element_type=F32)


def mm_nt(x, y):
    return lax.dot_general(x, y, (((1,), (1,)), ((), ())), preferred_element_type=F32)


def kernel(
    ranks, peers,
    q_ref, k_ref, v_ref, rate_ref, step_ref, wg_ref, wu_ref, wd_ref,
    out_ref,
    wdt, own, sib, low, high, xin, gram_b, xall, wnew, part, pin,
    sib_send, sib_recv, rs_send, low_recv, high_recv, hid_send, hid_recv,
    ag_sib, ag_low, ag_high, ag_recv, fr_send, fr_recv,
):
    heads, dh, units = wg_ref.shape
    problems = 3 * heads
    n = problems // 2
    zs = ranks // 2
    tok_rows = k_ref.shape[0]
    width = out_ref.shape[1]
    t = lax.axis_index("tok")
    h = lax.axis_index("hid")
    z = lax.div(t, 2)
    c = lax.rem(t, 2)
    pair = {"tok": 2 * z + 1 - c}
    below = {"tok": jnp.maximum(2 * (z - 1) + c, 0)}
    above = {"tok": jnp.minimum(2 * (z + 1) + c, ranks - 1)}

    def home(i):
        def at(core):
            return i if i < (n + 1 - core) // 2 else zs - n + i

        return at(0) + c * (at(1) - at(0))

    def copy(src, dst, send, recv, where):
        return pltpu.make_async_remote_copy(
            src_ref=src, dst_ref=dst, send_sem=send, recv_sem=recv,
            device_id=where, device_id_type=MESH,
        )

    def peer(k):
        return lax.rem(h + k, peers)

    barrier = pltpu.get_barrier_semaphore()
    pl.semaphore_signal(barrier, inc=1, device_id=pair, device_id_type=MESH)
    for k in range(1, peers):
        pl.semaphore_signal(barrier, inc=1, device_id={"hid": peer(k)}, device_id_type=MESH)

    @pl.when(z > 0)
    def _():
        pl.semaphore_signal(barrier, inc=1, device_id=below, device_id_type=MESH)

    @pl.when(z < zs - 1)
    def _():
        pl.semaphore_signal(barrier, inc=1, device_id=above, device_id_type=MESH)

    def greet():
        pl.semaphore_wait(
            barrier, peers + jnp.minimum(z, 1) + jnp.minimum(zs - 1 - z, 1)
        )

    def rows(ch):
        return pl.ds(ch * (dh // CHUNKS), dh // CHUNKS)

    def sib_copy(i):
        return copy(own.at[2 * i + 1 - c], sib.at[i], sib_send.at[i], sib_recv.at[i], pair)

    def up_copy(i, ch):
        return copy(
            own.at[2 * i + c, rows(ch)], low.at[i, rows(ch)],
            rs_send.at[i, ch], low_recv.at[i, ch], above,
        )

    def down_copy(i, ch):
        return copy(
            own.at[2 * i + c, rows(ch)], high.at[i, rows(ch)],
            rs_send.at[i, ch], high_recv.at[i, ch], below,
        )

    def chip_sum(i):
        sib_copy(i).wait_recv()
        own[2 * i + c] = (own[2 * i + c].astype(F32) + sib[i].astype(F32)).astype(BF16)

    def hop(i, s):
        @pl.when((z < home(i)) & (z == s))
        def _():
            for ch in range(CHUNKS):
                if s > 0:
                    up_copy(i, ch).wait_recv()
                    own[2 * i + c, rows(ch)] = (
                        own[2 * i + c, rows(ch)].astype(F32) + low[i, rows(ch)].astype(F32)
                    ).astype(BF16)
                up_copy(i, ch).start()

        @pl.when((z > home(i)) & (zs - 1 - z == s))
        def _():
            for ch in range(CHUNKS):
                if s > 0:
                    down_copy(i, ch).wait_recv()
                    own[2 * i + c, rows(ch)] = (
                        own[2 * i + c, rows(ch)].astype(F32) + high[i, rows(ch)].astype(F32)
                    ).astype(BF16)
                down_copy(i, ch).start()

    done = 0
    for head in range(heads):
        cols = slice(head * dh, (head + 1) * dh)
        wdt[head] = wd_ref[head].T
        keys = k_ref[:, cols]
        target = (-(rate_ref[:, head : head + 1] * v_ref[:, cols].astype(F32))).astype(BF16)
        gate_pre = mm(keys, wg_ref[head])
        up_pre = mm(keys, wu_ref[head])
        back = mm(target, wdt[head])
        sig = jax.nn.sigmoid(gate_pre)
        active = gate_pre * sig
        keys_t = keys.T
        grads = (
            (keys_t, (back * up_pre * sig * (1.0 + gate_pre * (1.0 - sig))).astype(BF16)),
            (keys_t, (back * active).astype(BF16)),
            (target.T, (active * up_pre).astype(BF16)),
        )
        for kind, (left, right) in enumerate(grads):
            p = 3 * head + kind
            own[p] = mm(left, right).astype(BF16)
            if p % 2 == 1:
                i = p // 2
                if i == 0:
                    greet()
                sib_copy(i).start()
                if i > 0:
                    chip_sum(i - 1)
                    hop(i - 1, 0)
    chip_sum(n - 1)
    hop(n - 1, 0)
    for s in range(1, zs):
        for i in range(n):
            hop(i, s)

    mine = 0
    has = 0
    for i in range(n):
        here = jnp.where(z == home(i), 1, 0)
        mine = mine + here * i
        has = has + here

    def hid_copy(k, ch, slot):
        return copy(
            xin.at[slot, rows(ch)], xin.at[slot, rows(ch)],
            hid_send.at[k, ch], hid_recv.at[slot, ch], {"hid": peer(k)},
        )

    @pl.when(has == 1)
    def _():
        for ch in range(CHUNKS):
            @pl.when(z > 0)
            def _():
                up_copy(mine, ch).wait_recv()
                own[2 * mine + c, rows(ch)] = (
                    own[2 * mine + c, rows(ch)].astype(F32) + low[mine, rows(ch)].astype(F32)
                ).astype(BF16)

            @pl.when(z < zs - 1)
            def _():
                down_copy(mine, ch).wait_recv()
                own[2 * mine + c, rows(ch)] = (
                    own[2 * mine + c, rows(ch)].astype(F32) + high[mine, rows(ch)].astype(F32)
                ).astype(BF16)

            xin[h, rows(ch)] = own[2 * mine + c, rows(ch)]
            for k in range(1, peers):
                hid_copy(k, ch, h).start()
        for k in range(1, peers):
            for ch in range(CHUNKS):
                hid_copy(k, ch, peer(k)).wait_recv()
        for k in range(1, peers):
            for ch in range(CHUNKS):
                hid_copy(k, ch, h).wait_send()
        squares = jnp.zeros((1, 1), F32)
        for j in range(peers):
            block = xin[j].astype(F32)
            squares = squares + jnp.sum(block * block).reshape(1, 1)
        inverse = 1.0 / (jnp.sqrt(squares) + 1e-07)
        gram = jnp.zeros((dh, dh), F32)
        for j in range(peers):
            block = (xin[j].astype(F32) * inverse).astype(BF16)
            xin[j] = block
            gram = gram + mm_nt(block, block)
        x = xin[h]
        for it in range(NS_ITERS):
            gram_b[...] = gram.astype(BF16)
            step = (poly_b * gram + poly_c * mm(gram_b[...], gram_b[...])).astype(BF16)
            x = (poly_a * x.astype(F32) + mm(step, x)).astype(BF16)
            if it < NS_ITERS - 1:
                half = poly_a * gram + mm(step, gram_b[...])
                gram = poly_a * half + mm(half.astype(BF16), step)
        xall[2 * mine + c] = x

    def ag_copy(i, ch, cls, sem, where):
        p = 2 * i + cls
        return copy(
            xall.at[p, rows(ch)], xall.at[p, rows(ch)], sem.at[i, ch], ag_recv.at[p, ch], where
        )

    for d in range(zs):
        for i in range(n):
            @pl.when(jnp.abs(z - home(i)) == d)
            def _():
                for ch in range(CHUNKS):
                    if d > 0:
                        ag_copy(i, ch, c, ag_sib, pair).wait_recv()

                    @pl.when((z <= home(i)) & (z > 0))
                    def _():
                        ag_copy(i, ch, c, ag_low, below).start()

                    @pl.when((z >= home(i)) & (z < zs - 1))
                    def _():
                        ag_copy(i, ch, c, ag_high, above).start()

                    ag_copy(i, ch, c, ag_sib, pair).start()
    for i in range(n):
        for ch in range(CHUNKS):
            ag_copy(i, ch, 1 - c, ag_sib, pair).wait_recv()

    for head in range(heads):
        rate = step_ref[:, head : head + 1]
        for kind, old_ref in enumerate((wg_ref, wu_ref, wdt)):
            old = old_ref[head].astype(F32)
            fresh = old - rate * xall[3 * head + kind].astype(F32)
            old_sq = jnp.sum(old * old, axis=0, keepdims=True)
            new_sq = jnp.sum(fresh * fresh, axis=0, keepdims=True)
            scale = jnp.sqrt(old_sq) / jnp.sqrt(new_sq + 1e-06)
            wnew[3 * head + kind] = (fresh * scale).astype(BF16)

    size = tok_rows // TOK_CHUNKS

    def fr_copy(j, tc, slot):
        span = pl.ds(tc * size, size)
        return copy(
            part.at[j, span], pin.at[slot, span], fr_send.at[j, tc], fr_recv.at[slot, tc],
            {"hid": j},
        )

    for tc in range(TOK_CHUNKS):
        span = slice(tc * size, (tc + 1) * size)
        for head in range(heads):
            query = q_ref[span, head * dh : (head + 1) * dh]
            gate = mm(query, wnew[3 * head])
            up = mm(query, wnew[3 * head + 1])
            hidden = (gate * jax.nn.sigmoid(gate) * up).astype(BF16)
            value = mm_nt(hidden, wnew[3 * head + 2]).astype(BF16)
            for b in range(dh // width):
                j = head * (dh // width) + b
                part[j, span] = value[:, b * width : (b + 1) * width]

                @pl.when(h != j)
                def _():
                    fr_copy(j, tc, h).start()
    for tc in range(TOK_CHUNKS):
        span = slice(tc * size, (tc + 1) * size)
        total = part[h, span].astype(F32)
        for k in range(1, peers):
            fr_copy(peer(k), tc, peer(k)).wait_recv()
            total = total + pin[peer(k), span].astype(F32)
        out_ref[span, :] = total.astype(BF16)

    for i in range(n):
        sib_copy(i).wait_send()
        for ch in range(CHUNKS):
            @pl.when(z != home(i))
            def _():
                up_copy(i, ch).wait_send()

            @pl.when((z <= home(i)) & (z > 0))
            def _():
                ag_copy(i, ch, c, ag_low, below).wait_send()

            @pl.when((z >= home(i)) & (z < zs - 1))
            def _():
                ag_copy(i, ch, c, ag_high, above).wait_send()

            ag_copy(i, ch, c, ag_sib, pair).wait_send()
    for k in range(1, peers):
        for tc in range(TOK_CHUNKS):
            fr_copy(peer(k), tc, h).wait_send()


def local(ranks, peers, queries, keys, values, token_rate, head_rate, w_gate, w_up, w_down):
    rows, all_cols = keys.shape
    heads, dh, units = w_gate.shape
    problems = 3 * heads
    n = problems // 2
    width = all_cols // peers
    dma = pltpu.SemaphoreType.DMA
    vmem = pl.BlockSpec(memory_space=pltpu.VMEM)
    return pl.pallas_call(
        functools.partial(kernel, ranks, peers),
        out_shape=jax.ShapeDtypeStruct((rows, width), BF16),
        in_specs=[vmem] * 8,
        out_specs=vmem,
        scratch_shapes=[
            pltpu.VMEM((heads, dh, units), BF16),
            pltpu.VMEM((problems, dh, units), BF16),
            pltpu.VMEM((n, dh, units), BF16),
            pltpu.VMEM((n, dh, units), BF16),
            pltpu.VMEM((n, dh, units), BF16),
            pltpu.VMEM((peers, dh, units), BF16),
            pltpu.VMEM((dh, dh), BF16),
            pltpu.VMEM((problems, dh, units), BF16),
            pltpu.VMEM((problems, dh, units), BF16),
            pltpu.VMEM((peers, rows, width), BF16),
            pltpu.VMEM((peers, rows, width), BF16),
            dma((n,)), dma((n,)),
            dma((n, CHUNKS)), dma((n, CHUNKS)), dma((n, CHUNKS)),
            dma((peers, CHUNKS)), dma((peers, CHUNKS)),
            dma((n, CHUNKS)), dma((n, CHUNKS)), dma((n, CHUNKS)),
            dma((problems, CHUNKS)),
            dma((peers, TOK_CHUNKS)), dma((peers, TOK_CHUNKS)),
        ],
        compiler_params=pltpu.CompilerParams(
            collective_id=0, has_side_effects=True, vmem_limit_bytes=56 * 1024 * 1024
        ),
    )(queries, keys, values, token_rate, head_rate.reshape(1, heads), w_gate, w_up, w_down)


def solution(mesh):
    return jax.shard_map(
        functools.partial(local, mesh.shape["tok"], mesh.shape["hid"]),
        mesh=mesh,
        in_specs=(
            P("tok", "head"),
            P("tok", "head"),
            P("tok", "head"),
            P("tok", "head"),
            P("head"),
            P("head", None, "hid"),
            P("head", None, "hid"),
            P("head", "hid", None),
        ),
        out_specs=P("tok", ("head", "hid")),
        check_vma=False,
    )
```

```python
import functools
import jax
import jax.numpy as jnp
from jax import lax
from jax.experimental import pallas as pl
from jax.experimental.pallas import tpu as pltpu
from jax.sharding import PartitionSpec as P

NS_ITERS = 3
poly_a = 3.4445
poly_b = -4.775
poly_c = 2.0315
CHUNKS = 4
TOK_CHUNKS = 2
F32 = jnp.float32
BF16 = jnp.bfloat16
MESH = pl.DeviceIdType.MESH


def mm(x, y):
    return jnp.dot(x, y, preferred_element_type=F32)


def mm_nt(x, y):
    return lax.dot_general(x, y, (((1,), (1,)), ((), ())), preferred_element_type=F32)


def kernel(
    ranks, peers,
    q_ref, k_ref, v_ref, rate_ref, step_ref, wg_ref, wu_ref, wd_ref,
    out_ref,
    wdt, own, sib, low, high, xin, gram_b, xall, wnew, part, pin,
    sib_send, sib_recv, rs_send, low_recv, high_recv, hid_send, hid_recv,
    ag_sib, ag_low, ag_high, ag_recv, fr_send, fr_recv,
):
    heads, dh, units = wg_ref.shape
    problems = 3 * heads
    n = problems // 2
    zs = ranks // 2
    tok_rows = k_ref.shape[0]
    width = out_ref.shape[1]
    t = lax.axis_index("tok")
    h = lax.axis_index("hid")
    z = lax.div(t, 2)
    c = lax.rem(t, 2)
    pair = {"tok": 2 * z + 1 - c}
    below = {"tok": jnp.maximum(2 * (z - 1) + c, 0)}
    above = {"tok": jnp.minimum(2 * (z + 1) + c, ranks - 1)}

    def home(i):
        def at(core):
            return i if i < (n + 1 - core) // 2 else zs - n + i

        return at(0) + c * (at(1) - at(0))

    def copy(src, dst, send, recv, where):
        return pltpu.make_async_remote_copy(
            src_ref=src, dst_ref=dst, send_sem=send, recv_sem=recv,
            device_id=where, device_id_type=MESH,
        )

    def peer(k):
        return lax.rem(h + k, peers)

    def mate(k):
        if peers != 4:
            return peer(k)
        one = 1 - 2 * lax.rem(h, 2)
        two = 2 - 4 * lax.div(h, 2)
        return h + (k % 2) * one + (k // 2) * two

    barrier = pltpu.get_barrier_semaphore()
    pl.semaphore_signal(barrier, inc=1, device_id=pair, device_id_type=MESH)
    for k in range(1, peers):
        pl.semaphore_signal(barrier, inc=1, device_id={"hid": peer(k)}, device_id_type=MESH)

    @pl.when(z > 0)
    def _():
        pl.semaphore_signal(barrier, inc=1, device_id=below, device_id_type=MESH)

    @pl.when(z < zs - 1)
    def _():
        pl.semaphore_signal(barrier, inc=1, device_id=above, device_id_type=MESH)

    def greet():
        pl.semaphore_wait(
            barrier, peers + jnp.minimum(z, 1) + jnp.minimum(zs - 1 - z, 1)
        )

    def rows(ch):
        return pl.ds(ch * (dh // CHUNKS), dh // CHUNKS)

    def sib_copy(i):
        return copy(own.at[2 * i + 1 - c], sib.at[i], sib_send.at[i], sib_recv.at[i], pair)

    def up_copy(i, ch):
        return copy(
            own.at[2 * i + c, rows(ch)], low.at[i, rows(ch)],
            rs_send.at[i, ch], low_recv.at[i, ch], above,
        )

    def down_copy(i, ch):
        return copy(
            own.at[2 * i + c, rows(ch)], high.at[i, rows(ch)],
            rs_send.at[i, ch], high_recv.at[i, ch], below,
        )

    def chip_sum(i):
        sib_copy(i).wait_recv()
        own[2 * i + c] = (own[2 * i + c].astype(F32) + sib[i].astype(F32)).astype(BF16)

    def hop(i, s):
        @pl.when((z < home(i)) & (z == s))
        def _():
            for ch in range(CHUNKS):
                if s > 0:
                    up_copy(i, ch).wait_recv()
                    own[2 * i + c, rows(ch)] = (
                        own[2 * i + c, rows(ch)].astype(F32) + low[i, rows(ch)].astype(F32)
                    ).astype(BF16)
                up_copy(i, ch).start()

        @pl.when((z > home(i)) & (zs - 1 - z == s))
        def _():
            for ch in range(CHUNKS):
                if s > 0:
                    down_copy(i, ch).wait_recv()
                    own[2 * i + c, rows(ch)] = (
                        own[2 * i + c, rows(ch)].astype(F32) + high[i, rows(ch)].astype(F32)
                    ).astype(BF16)
                down_copy(i, ch).start()

    done = 0
    for head in range(heads):
        cols = slice(head * dh, (head + 1) * dh)
        wdt[head] = wd_ref[head].T
        keys = k_ref[:, cols]
        target = (-(rate_ref[:, head : head + 1] * v_ref[:, cols].astype(F32))).astype(BF16)
        gate_pre = mm(keys, wg_ref[head])
        up_pre = mm(keys, wu_ref[head])
        back = mm(target, wdt[head])
        sig = jax.nn.sigmoid(gate_pre)
        active = gate_pre * sig
        keys_t = keys.T
        grads = (
            (keys_t, (back * up_pre * sig * (1.0 + gate_pre * (1.0 - sig))).astype(BF16)),
            (keys_t, (back * active).astype(BF16)),
            (target.T, (active * up_pre).astype(BF16)),
        )
        for kind, (left, right) in enumerate(grads):
            p = 3 * head + kind
            own[p] = mm(left, right).astype(BF16)
            if p % 2 == 1:
                i = p // 2
                if i == 0:
                    greet()
                sib_copy(i).start()
                if i > 0:
                    chip_sum(i - 1)
                    hop(i - 1, 0)
    chip_sum(n - 1)
    hop(n - 1, 0)
    for s in range(1, zs):
        for i in range(n):
            hop(i, s)

    mine = 0
    has = 0
    for i in range(n):
        here = jnp.where(z == home(i), 1, 0)
        mine = mine + here * i
        has = has + here

    def hid_copy(k, ch, slot):
        return copy(
            xin.at[slot, rows(ch)], xin.at[slot, rows(ch)],
            hid_send.at[k, ch], hid_recv.at[slot, ch], {"hid": mate(k)},
        )

    @pl.when(has == 1)
    def _():
        for ch in range(CHUNKS):
            @pl.when(z > 0)
            def _():
                up_copy(mine, ch).wait_recv()
                own[2 * mine + c, rows(ch)] = (
                    own[2 * mine + c, rows(ch)].astype(F32) + low[mine, rows(ch)].astype(F32)
                ).astype(BF16)

            @pl.when(z < zs - 1)
            def _():
                down_copy(mine, ch).wait_recv()
                own[2 * mine + c, rows(ch)] = (
                    own[2 * mine + c, rows(ch)].astype(F32) + high[mine, rows(ch)].astype(F32)
                ).astype(BF16)

            xin[h, rows(ch)] = own[2 * mine + c, rows(ch)]
            for k in range(1, peers):
                if k < 3 or peers != 4:
                    hid_copy(k, ch, h).start()
        if peers == 4:
            for ch in range(CHUNKS):
                near = 1 + ch % 2
                hid_copy(near, ch, mate(near)).wait_recv()
                copy(
                    xin.at[mate(near), rows(ch)], xin.at[mate(near), rows(ch)],
                    hid_send.at[3, ch], hid_recv.at[mate(near), ch], {"hid": mate(3 - near)},
                ).start()
            for ch in range(CHUNKS):
                far = 2 - ch % 2
                hid_copy(far, ch, mate(far)).wait_recv()
                hid_copy(3, ch, mate(3)).wait_recv()
        else:
            for k in range(1, peers):
                for ch in range(CHUNKS):
                    hid_copy(k, ch, mate(k)).wait_recv()
        for k in range(1, peers):
            for ch in range(CHUNKS):
                hid_copy(k, ch, h).wait_send()
        squares = jnp.zeros((1, 1), F32)
        for j in range(peers):
            block = xin[j].astype(F32)
            squares = squares + jnp.sum(block * block).reshape(1, 1)
        inverse = 1.0 / (jnp.sqrt(squares) + 1e-07)
        gram = jnp.zeros((dh, dh), F32)
        for j in range(peers):
            block = (xin[j].astype(F32) * inverse).astype(BF16)
            xin[j] = block
            gram = gram + mm_nt(block, block)
        x = xin[h]
        for it in range(NS_ITERS):
            gram_b[...] = gram.astype(BF16)
            step = (poly_b * gram + poly_c * mm(gram_b[...], gram_b[...])).astype(BF16)
            x = (poly_a * x.astype(F32) + mm(step, x)).astype(BF16)
            if it < NS_ITERS - 1:
                half = poly_a * gram + mm(step, gram_b[...])
                gram = poly_a * half + mm(half.astype(BF16), step)
        xall[2 * mine + c] = x

    def ag_copy(i, ch, cls, sem, where):
        p = 2 * i + cls
        return copy(
            xall.at[p, rows(ch)], xall.at[p, rows(ch)], sem.at[i, ch], ag_recv.at[p, ch], where
        )

    def ag_round(d):
        for i in range(n):
            @pl.when(jnp.abs(z - home(i)) == d)
            def _():
                for ch in range(CHUNKS):
                    if d > 0:
                        ag_copy(i, ch, c, ag_sib, pair).wait_recv()

                    @pl.when((z <= home(i)) & (z > 0))
                    def _():
                        ag_copy(i, ch, c, ag_low, below).start()

                    @pl.when((z >= home(i)) & (z < zs - 1))
                    def _():
                        ag_copy(i, ch, c, ag_high, above).start()

                    ag_copy(i, ch, c, ag_sib, pair).start()

    def renew(head):
        rate = jnp.where(head == 0, step_ref[:, 0:1], step_ref[:, heads - 1 : heads])
        if heads > 2:
            for other in range(1, heads - 1):
                rate = jnp.where(head == other, step_ref[:, other : other + 1], rate)
        for kind, old_ref in enumerate((wg_ref, wu_ref, wdt)):
            p = 3 * head + kind

            @pl.when(lax.rem(p, 2) != c)
            def _():
                for ch in range(CHUNKS):
                    copy(
                        xall.at[p, rows(ch)], xall.at[p, rows(ch)],
                        ag_sib.at[0, ch], ag_recv.at[p, ch], pair,
                    ).wait_recv()

            old = old_ref[head].astype(F32)
            fresh = old - rate * xall[p].astype(F32)
            old_sq = jnp.sum(old * old, axis=0, keepdims=True)
            new_sq = jnp.sum(fresh * fresh, axis=0, keepdims=True)
            scale = jnp.sqrt(old_sq) / jnp.sqrt(new_sq + 1e-06)
            wnew[kind] = (fresh * scale).astype(BF16)

    size = tok_rows // TOK_CHUNKS
    wide = dh // width

    def span_of(tc):
        return pl.ds(tc * size, size)

    def fr_copy(j, tc, slot):
        return copy(
            part.at[j, span_of(tc)], pin.at[slot, span_of(tc)],
            fr_send.at[j, tc], fr_recv.at[slot, tc], {"hid": j},
        )

    def first_copy(head, tc):
        return copy(
            part.at[2 * head + 1 - lax.rem(h, 2), span_of(tc)], pin.at[head, span_of(tc)],
            fr_send.at[head, tc], fr_recv.at[head, tc], {"hid": mate(1)},
        )

    def second_copy(tc):
        j = mate(2)
        return copy(
            part.at[j, span_of(tc)], pin.at[2, span_of(tc)],
            fr_send.at[2, tc], fr_recv.at[2, tc], {"hid": j},
        )

    def terms(head):
        renew(head)
        for tc in range(TOK_CHUNKS):
            cols = pl.ds(pl.multiple_of(head * dh, dh), dh)
            query = q_ref[tc * size : (tc + 1) * size, cols]
            gate = mm(query, wnew[0])
            up = mm(query, wnew[1])
            hidden = (gate * jax.nn.sigmoid(gate) * up).astype(BF16)
            value = mm_nt(hidden, wnew[2]).astype(BF16)
            for b in range(wide):
                j = head * wide + b
                part[j, span_of(tc)] = value[:, b * width : (b + 1) * width]
                if not paired:
                    @pl.when(h != j)
                    def _():
                        fr_copy(j, tc, h).start()
            if paired:
                first_copy(head, tc).start()

    def second(head):
        j = 2 * head + lax.rem(h, 2)
        for tc in range(TOK_CHUNKS):
            first_copy(head, tc).wait_recv()
            part[j, span_of(tc)] = (
                part[j, span_of(tc)].astype(F32) + pin[head, span_of(tc)].astype(F32)
            ).astype(BF16)

            @pl.when(h != j)
            def _():
                second_copy(tc).start()

    paired = peers == 4 and heads == 2 and wide == 2
    if paired:
        end = (z == 0) | (z == zs - 1)
        inner = (z > 0) & (z < zs - 1)
        near = jnp.where(z < zs // 2, 0, 1)
        for d in range(min(2, zs)):
            ag_round(d)

        @pl.when(inner)
        def _():
            for d in range(2, zs):
                ag_round(d)

        terms(near)

        @pl.when(end)
        def _():
            second(near)
            for d in range(2, zs):
                ag_round(d)

        terms(1 - near)

        @pl.when(inner)
        def _():
            second(near)

        second(1 - near)
        for tc in range(TOK_CHUNKS):
            second_copy(tc).wait_recv()
            out_ref[tc * size : (tc + 1) * size, :] = (
                part[h, span_of(tc)].astype(F32) + pin[2, span_of(tc)].astype(F32)
            ).astype(BF16)
        for tc in range(TOK_CHUNKS):
            for head in range(heads):
                first_copy(head, tc).wait_send()
            second_copy(tc).wait_send()
    else:
        for d in range(zs):
            ag_round(d)
        for head in range(heads):
            terms(head)
        for tc in range(TOK_CHUNKS):
            total = part[h, span_of(tc)].astype(F32)
            for k in range(1, peers):
                fr_copy(peer(k), tc, peer(k)).wait_recv()
                total = total + pin[peer(k), span_of(tc)].astype(F32)
            out_ref[tc * size : (tc + 1) * size, :] = total.astype(BF16)
        for k in range(1, peers):
            for tc in range(TOK_CHUNKS):
                fr_copy(peer(k), tc, h).wait_send()

    for i in range(n):
        sib_copy(i).wait_send()
        for ch in range(CHUNKS):
            @pl.when(z != home(i))
            def _():
                up_copy(i, ch).wait_send()

            @pl.when((z <= home(i)) & (z > 0))
            def _():
                ag_copy(i, ch, c, ag_low, below).wait_send()

            @pl.when((z >= home(i)) & (z < zs - 1))
            def _():
                ag_copy(i, ch, c, ag_high, above).wait_send()

            ag_copy(i, ch, c, ag_sib, pair).wait_send()


def local(ranks, peers, queries, keys, values, token_rate, head_rate, w_gate, w_up, w_down):
    rows, all_cols = keys.shape
    heads, dh, units = w_gate.shape
    problems = 3 * heads
    n = problems // 2
    width = all_cols // peers
    dma = pltpu.SemaphoreType.DMA
    vmem = pl.BlockSpec(memory_space=pltpu.VMEM)
    return pl.pallas_call(
        functools.partial(kernel, ranks, peers),
        out_shape=jax.ShapeDtypeStruct((rows, width), BF16),
        in_specs=[vmem] * 8,
        out_specs=vmem,
        scratch_shapes=[
            pltpu.VMEM((heads, dh, units), BF16),
            pltpu.VMEM((problems, dh, units), BF16),
            pltpu.VMEM((n, dh, units), BF16),
            pltpu.VMEM((n, dh, units), BF16),
            pltpu.VMEM((n, dh, units), BF16),
            pltpu.VMEM((peers, dh, units), BF16),
            pltpu.VMEM((dh, dh), BF16),
            pltpu.VMEM((problems, dh, units), BF16),
            pltpu.VMEM((3, dh, units), BF16),
            pltpu.VMEM((peers, rows, width), BF16),
            pltpu.VMEM((peers, rows, width), BF16),
            dma((n,)), dma((n,)),
            dma((n, CHUNKS)), dma((n, CHUNKS)), dma((n, CHUNKS)),
            dma((peers, CHUNKS)), dma((peers, CHUNKS)),
            dma((n, CHUNKS)), dma((n, CHUNKS)), dma((n, CHUNKS)),
            dma((problems, CHUNKS)),
            dma((peers, TOK_CHUNKS)), dma((peers, TOK_CHUNKS)),
        ],
        compiler_params=pltpu.CompilerParams(
            collective_id=0, has_side_effects=True, vmem_limit_bytes=56 * 1024 * 1024
        ),
    )(queries, keys, values, token_rate, head_rate.reshape(1, heads), w_gate, w_up, w_down)


def solution(mesh):
    return jax.shard_map(
        functools.partial(local, mesh.shape["tok"], mesh.shape["hid"]),
        mesh=mesh,
        in_specs=(
            P("tok", "head"),
            P("tok", "head"),
            P("tok", "head"),
            P("tok", "head"),
            P("head"),
            P("head", None, "hid"),
            P("head", None, "hid"),
            P("head", "hid", None),
        ),
        out_specs=P("tok", ("head", "hid")),
        check_vma=False,
    )
```
